32 devices in a mesh: gx: 4 (over z), gy: 2 (over y), gz: 4 (over x, core).
Axes of the slice: x: 2, y: 2, z: 4, core: 2. Of those that a mesh axis runs over, the one named last changes fastest.
Arguments:
- populations: float32 [19, 16, 32, 1024], P(None, None, ('gy', 'gz'), 'gx'), may hold values from 0 to 0.5, as said below
- cell_type: int32 [16, 32, 1024], P(None, ('gy', 'gz'), 'gx'), may hold values from 0 to 2, as said below
- adjoint: float32 [7, 16, 32, 1024], P(None, 'gz', 'gy', 'gx'), may hold values from -6 to 6
Outputs:
- flow_next: float32 [19, 16, 32, 1024], P(None, None, ('gy', 'gz'), 'gx')
- adjoint_prev: float32 [7, 16, 32, 1024], P(None, 'gz', 'gy', 'gx')
The draws below stay inside these ranges and needn't reach their ends.
Inputs may be any that keep to these rules, and one draw needn't show every extreme that they name: `cell_type`: layers below 8 are solid (code 1), with code 2 cells only in layer 0; layers from 8 on hold codes 0 and 1, and a cell's code is the same in all of them. `populations`: each population is its lattice weight times a positive factor near one.
All inputs are finite; a program needn't handle non-finite values.
Results may differ from the reference program's by a relative error of at most 0.000065.
Values sent between devices are 32-bit elements; how exact they have to be, the bound alone decides.
A program may use at most 64 MiB of HBM per device.

```python
import jax
import jax.numpy as jnp
from jax import lax

BASE = 8
DEPTH = 16
ROWS = 32
CELLS_X = 1024


WEIGHT_TABLE = [1.0 / 3.0] + [1.0 / 18.0] * 6 + [1.0 / 36.0] * 12


DRIFT_TABLE = [1.0, 1.1, 0.9, 1.0, 1.0, 1.0, 1.0, 1.1, 0.9, 1.1, 0.9, 1.1, 0.9, 1.1, 0.9, 1.0, 1.0, 1.0, 1.0]


def draw_populations(key, part):
    shape = (19, DEPTH, ROWS, CELLS_X)
    factor = 1.0 + 0.1 * jax.random.truncated_normal(key, -2.5, 2.5, shape, jnp.float32)
    scale = jnp.array(WEIGHT_TABLE, jnp.float32) * jnp.array(DRIFT_TABLE, jnp.float32)
    return scale[:, None, None, None] * factor


def draw_cell_type(key, part):
    key_pin, key_heat = jax.random.split(jax.random.fold_in(key, 11))
    pillar = jax.random.randint(key_pin, (ROWS, CELLS_X), 0, 10) < 3
    heated = jax.random.randint(key_heat, (ROWS, CELLS_X), 0, 4) == 0
    layer = jnp.arange(DEPTH)[:, None, None]
    base = jnp.where((layer == 0) & heated[None], 2, 1)
    upper = jnp.where(pillar[None], 1, 0)
    return jnp.where(layer < BASE, base, upper).astype(jnp.int32)


def level_of(stream_key, extent, shards, low, top_value):
    level, own = 1.0, jax.random.fold_in(stream_key, 6)
    for axis_at, parts in shards:
        draws = jnp.exp(jax.random.uniform(jax.random.fold_in(own, axis_at), (parts,), jnp.float32, low / len(shards), top_value / len(shards)))
        level = level * jnp.repeat(draws, extent[axis_at] // parts).reshape([-1 if axis == axis_at else 1 for axis in range(len(extent))])
    return level


def noise(key, dims, deviation, most, shards=(), held_as=jnp.bfloat16):
    entries = jax.random.normal(key, dims, jnp.float32) * deviation
    if len(shards) > 0:
        entries = level_of(key, dims, shards, -0.22, 0.18) * entries
    return jnp.clip(entries, min=-most, max=most).astype(held_as)


def setup_inputs(seed: int = 0) -> dict:
    streams_of = jax.random.split(jax.random.key(seed), 4)
    populations = draw_populations(jax.random.fold_in(streams_of[3], 71), 0)
    cell_type = draw_cell_type(jax.random.fold_in(streams_of[3], 71), 0)
    adjoint = noise(streams_of[2], (7, DEPTH, ROWS, CELLS_X), 1.0, 6.0, ((1, 4), (2, 2), (3, 4)), jnp.float32)
    return {"populations": populations, "cell_type": cell_type, "adjoint": adjoint}


VEL19 = [(0, 0, 0), (1, 0, 0), (-1, 0, 0), (0, 1, 0), (0, -1, 0), (0, 0, 1), (0, 0, -1),
         (1, 1, 0), (-1, -1, 0), (1, -1, 0), (-1, 1, 0), (1, 0, 1), (-1, 0, -1), (1, 0, -1), (-1, 0, 1),
         (0, 1, 1), (0, -1, -1), (0, 1, -1), (0, -1, 1)]
WEIGHT19 = [1.0 / 3.0] + [1.0 / 18.0] * 6 + [1.0 / 36.0] * 12
OPPOSITE = [0, 2, 1, 4, 3, 6, 5, 8, 7, 10, 9, 12, 11, 14, 13, 16, 15, 18, 17]
VEL7 = [(0, 0, 0), (1, 0, 0), (-1, 0, 0), (0, 1, 0), (0, -1, 0), (0, 0, 1), (0, 0, -1)]
WEIGHT7 = [0.25] + [0.125] * 6
OMEGA_FLOW = 1.6
OMEGA_FLUID = 1.25
OMEGA_SOLID = 1.6


def moments(pops):
    table = jnp.array(VEL19, jnp.float32).T
    density = jnp.sum(pops, axis=0)
    momentum = jnp.tensordot(table, pops, axes=1, precision=lax.Precision.HIGHEST)
    return density, momentum / density


def collide(pops):
    density, velocity = moments(pops)
    usq = jnp.sum(velocity * velocity, axis=0)
    outs = []
    for i in range(19):
        cx, cy, cz = VEL19[i]
        cu = cx * velocity[0] + cy * velocity[1] + cz * velocity[2]
        feq = WEIGHT19[i] * density * (1.0 + 3.0 * cu + 4.5 * cu * cu - 1.5 * usq)
        outs.append(pops[i] - OMEGA_FLOW * (pops[i] - feq))
    return jnp.stack(outs)


def stream(padded, post, pops, fluid):
    depth, rows, cols = fluid.shape
    outs = []
    for i in range(19):
        cx, cy, cz = VEL19[i]
        src = padded[i, 1 - cz:1 - cz + depth, 1 - cy:1 - cy + rows, 1 - cx:1 - cx + cols]
        flag = padded[19, 1 - cz:1 - cz + depth, 1 - cy:1 - cy + rows, 1 - cx:1 - cx + cols]
        pulled = flag * src + (1.0 - flag) * post[OPPOSITE[i]]
        outs.append(jnp.where(fluid > 0.5, pulled, pops[i]))
    return jnp.stack(outs)


def thermal(padded, velocity, codes):
    depth, rows, cols = codes.shape
    pulled = []
    for j in range(7):
        ex, ey, ez = VEL7[j]
        pulled.append(padded[j, 1 + ez:1 + ez + depth, 1 + ey:1 + ey + rows, 1 + ex:1 + ex + cols])
    mean_term = sum(WEIGHT7[j] * pulled[j] for j in range(7))
    flux = [sum(WEIGHT7[j] * VEL7[j][k] * pulled[j] for j in range(7)) for k in range(3)]
    coupled = mean_term + 4.0 * (velocity[0] * flux[0] + velocity[1] * flux[1] + velocity[2] * flux[2])
    omega = jnp.where(codes == 0.0, OMEGA_FLUID, OMEGA_SOLID)
    source = jnp.where(codes == 2.0, 1.0, 0.0)
    return jnp.stack([(1.0 - omega) * pulled[j] + omega * coupled + source for j in range(7)])


def reference(populations, cell_type, adjoint):
    fluid = jnp.where(cell_type == 0, 1.0, 0.0).astype(jnp.float32)
    post = collide(populations)
    stacked = jnp.concatenate([post, fluid[None]], axis=0)
    padded = jnp.pad(stacked, ((0, 0), (1, 1), (1, 1), (1, 1)))
    flow_next = stream(padded, post, populations, fluid)
    density = jnp.sum(flow_next, axis=0)
    table = jnp.array(VEL19, jnp.float32).T
    velocity = jnp.tensordot(table, flow_next, axes=1, precision=lax.Precision.HIGHEST) / density * fluid
    codes = cell_type.astype(jnp.float32)
    heat_pad = jnp.pad(adjoint, ((0, 0), (1, 1), (1, 1), (1, 1)))
    adjoint_prev = thermal(heat_pad, velocity, codes)
    return flow_next, adjoint_prev
```

```python
import functools

import jax
import jax.numpy as jnp
from jax import lax
from jax.experimental import pallas as pl
from jax.experimental.pallas import tpu as pltpu
from jax.sharding import PartitionSpec as P

VEL19 = [
    (0, 0, 0), (1, 0, 0), (-1, 0, 0), (0, 1, 0), (0, -1, 0), (0, 0, 1), (0, 0, -1),
    (1, 1, 0), (-1, -1, 0), (1, -1, 0), (-1, 1, 0), (1, 0, 1), (-1, 0, -1), (1, 0, -1),
    (-1, 0, 1), (0, 1, 1), (0, -1, -1), (0, 1, -1), (0, -1, 1),
]
WEIGHT19 = [1.0 / 3.0] + [1.0 / 18.0] * 6 + [1.0 / 36.0] * 12
OPPOSITE = [0, 2, 1, 4, 3, 6, 5, 8, 7, 10, 9, 12, 11, 14, 13, 16, 15, 18, 17]
OMEGA_FLOW = 1.6
OMEGA_FLUID = 1.25
OMEGA_SOLID = 1.6
BASE = 8
LANES = 128
MESH = pl.DeviceIdType.MESH

RIGHT = [1, 7, 9, 11, 13]
LEFT = [2, 8, 10, 12, 14]
UP = [7, 10, 3, 15, 17]
DOWN = [8, 9, 4, 16, 18]


def tree_sum(terms):
    terms = list(terms)
    while len(terms) > 1:
        terms = [sum(terms[i : i + 2][1:], terms[i]) for i in range(0, len(terms), 2)]
    return terms[0]


def momentum(pops):
    out = []
    for k in range(3):
        plus = tree_sum([pops[i] for i in range(19) if VEL19[i][k] > 0])
        minus = tree_sum([pops[i] for i in range(19) if VEL19[i][k] < 0])
        out.append(plus - minus)
    return out


def kernel(
    sizes, pops_hbm, cell_hbm, adj_hbm, flow_hbm, prev_hbm,
    pops, cells, adj, post, flags, prev,
    xs, xr, ys, yr, ds, tx, ty, tz, vel, vin, heat, hin,
    in_sem, out_sem, send_sem, recv_sem, tsend, trecv, vsend, vrecv, hsend, hrecv, vloc,
):
    ngx, ngy, ngz, depth, rows, cols = sizes
    layers = depth - BASE
    thick = depth // ngz
    solid_ranks = BASE // thick
    gx, gy, gz = lax.axis_index("gx"), lax.axis_index("gy"), lax.axis_index("gz")
    band = gy * ngz + gz
    nband = ngy * ngz

    def at(x, b):
        return {"gx": x, "gy": b // ngz, "gz": lax.rem(b, ngz)}

    has = {
        (1, 0): gx < ngx - 1, (-1, 0): gx > 0,
        (0, 1): band < nband - 1, (0, -1): band > 0,
    }
    for dx in (1, -1):
        for dy in (1, -1):
            has[dx, dy] = jnp.logical_and(has[dx, 0], has[0, dy])
    where_to = {key: at(gx + key[0], band + key[1]) for key in has}
    thermal_links = [
        (gx < ngx - 1, {"gx": gx + 1, "gy": gy, "gz": gz}),
        (gx > 0, {"gx": gx - 1, "gy": gy, "gz": gz}),
        (gy < ngy - 1, {"gx": gx, "gy": gy + 1, "gz": gz}),
        (gy > 0, {"gx": gx, "gy": gy - 1, "gz": gz}),
        (gz < ngz - 1, {"gx": gx, "gy": gy, "gz": gz + 1}),
        (gz > 0, {"gx": gx, "gy": gy, "gz": gz - 1}),
    ]
    peers = [{"gx": gx, "gy": gy, "gz": lax.rem(gz + k, ngz)} for k in range(1, ngz)]

    load_pops = pltpu.make_async_copy(pops_hbm.at[:, pl.ds(BASE, layers)], pops, in_sem.at[0])
    load_top = pltpu.make_async_copy(cell_hbm.at[pl.ds(BASE, 1)], cells.at[pl.ds(0, 1)], in_sem.at[1])
    load_low = pltpu.make_async_copy(cell_hbm.at[pl.ds(0, 1)], cells.at[pl.ds(1, 1)], in_sem.at[2])
    load_adj = pltpu.make_async_copy(adj_hbm, adj, in_sem.at[3])
    keep_low = pltpu.make_async_copy(
        pops_hbm.at[:, pl.ds(0, BASE)], flow_hbm.at[:, pl.ds(0, BASE)], out_sem.at[0]
    )
    load_pops.start()
    load_top.start()
    load_low.start()
    load_adj.start()
    keep_low.start()

    barrier = pltpu.get_barrier_semaphore()
    total = jnp.int32(ngz - 1)
    for peer in peers:
        pl.semaphore_signal(barrier, inc=1, device_id=peer, device_id_type=MESH)
    links = [(has[key], where_to[key]) for key in has] + thermal_links[2:4]
    for ok, target in links:
        @pl.when(ok)
        def _():
            pl.semaphore_signal(barrier, inc=1, device_id=target, device_id_type=MESH)
        total = total + ok.astype(jnp.int32)

    load_top.wait()
    load_low.wait()
    load_pops.wait()
    own_flag = jnp.where(cells[0] == 0, 1.0, 0.0)
    flags[0:rows, 0:cols] = own_flag
    heat[0] = cells[1].astype(jnp.float32)
    ys[0, layers] = own_flag[rows - 1 :]
    ys[1, layers] = own_flag[:1]
    lane = lax.broadcasted_iota(jnp.int32, (8, LANES), 1)

    def collide(l, carry):
        p = [pops[i, l] for i in range(19)]
        rho = tree_sum(p)
        m = momentum(p)
        inv = 1.0 / rho
        base = rho - 1.5 * (m[0] * m[0] + m[1] * m[1] + m[2] * m[2]) * inv
        inv45 = 4.5 * inv
        q = [None] * 19
        q[0] = (1.0 - OMEGA_FLOW) * p[0] + (OMEGA_FLOW * WEIGHT19[0]) * base
        for i in range(1, 19, 2):
            cm = tree_sum([m[k] if VEL19[i][k] > 0 else -m[k] for k in range(3) if VEL19[i][k]])
            even = base + inv45 * cm * cm
            odd = 3.0 * cm
            w = OMEGA_FLOW * WEIGHT19[i]
            q[i] = (1.0 - OMEGA_FLOW) * p[i] + w * (even + odd)
            q[i + 1] = (1.0 - OMEGA_FLOW) * p[i + 1] + w * (even - odd)
        for i in range(19):
            post[i, l + 1, 0:rows, 0:cols] = q[i]
        for side, (names, row) in enumerate(((UP, rows - 1), (DOWN, 0))):
            for k, i in enumerate(names):
                ys[side, l + k * layers + (1 if k else 0)] = q[i][row : row + 1]
        for side, names in enumerate((RIGHT, LEFT)):
            first = cols - LANES if side == 0 else 0
            edge = 1 if side == 0 else 0
            packed = jnp.zeros((8, LANES), jnp.float32)
            for k, i in enumerate(names):
                tile = post[i, l + 1, :, first : first + LANES]
                packed = jnp.where(lane == k, pltpu.roll(tile, (k + edge) % LANES, 1), packed)
            tile = flags[:, first : first + LANES]
            k = len(names)
            packed = jnp.where(lane == k, pltpu.roll(tile, (k + edge) % LANES, 1), packed)
            xs[side, l] = packed[0:rows]
        return carry

    lax.fori_loop(0, layers, collide, 0)

    pl.semaphore_wait(barrier, total)

    def remote(src, dst, ssem, rsem, target):
        return pltpu.make_async_remote_copy(
            src_ref=src, dst_ref=dst, send_sem=ssem, recv_sem=rsem,
            device_id=target, device_id_type=MESH,
        )

    last = pl.ds(cols - LANES, LANES)
    lead = pl.ds(0, LANES)
    jobs = [
        ((1, 0), xs.at[0], xr.at[0]),
        ((-1, 0), xs.at[1], xr.at[1]),
        ((0, 1), ys.at[0], yr.at[0]),
        ((0, -1), ys.at[1], yr.at[1]),
        ((1, 1), ys.at[0, pl.ds(0, layers + 1), :, last], ds.at[0]),
        ((-1, 1), ys.at[0, pl.ds(layers, layers + 1), :, lead], ds.at[1]),
        ((-1, -1), ys.at[1, pl.ds(0, layers + 1), :, lead], ds.at[2]),
        ((1, -1), ys.at[1, pl.ds(layers, layers + 1), :, last], ds.at[3]),
    ]
    flow_copies = []
    for n, (way, src, dst) in enumerate(jobs):
        copy = remote(src, dst, send_sem.at[n], recv_sem.at[n], where_to[way])
        flow_copies.append((copy, has[way], has[-way[0], -way[1]]))
    for copy, ok, _ in flow_copies:
        pl.when(ok)(copy.start)

    tcopies = []
    tjobs = [
        (1, adj_hbm.at[2, :, :, last], tx.at[1], 0),
        (0, adj_hbm.at[1, :, :, lead], tx.at[0], 1),
        (3, adj_hbm.at[4, :, pl.ds(adj.shape[2] - 8, 8), :], ty.at[1], 2),
        (2, adj_hbm.at[3, :, pl.ds(0, 8), :], ty.at[0], 3),
        (5, adj_hbm.at[6, thick - 1], tz.at[1], 4),
        (4, adj_hbm.at[5, 0], tz.at[0], 5),
    ]
    for sem, src, dst, link in tjobs:
        copy = remote(src, dst, tsend.at[sem], trecv.at[sem], thermal_links[link][1])
        tcopies.append((copy, thermal_links[link][0], thermal_links[link ^ 1][0], dst))
    for copy, ok, _, _ in tcopies:
        pl.when(ok)(copy.start)
    heat_send = remote(heat, hin.at[gz], hsend, hrecv.at[gz], {"gx": gx, "gy": gy, "gz": 0})
    pl.when(gz > 0)(heat_send.start)

    for n, (copy, _, ok) in enumerate(flow_copies):
        pl.when(ok)(copy.wait_recv)

        @pl.when(jnp.logical_not(ok))
        def _():
            if n < 2:
                xr[n, 0] = jnp.zeros((rows, LANES), jnp.float32)
            elif n < 4:
                yr[n - 2, layers] = jnp.zeros((1, cols), jnp.float32)
            else:
                ds[n - 4, layers if n % 2 == 0 else 0] = jnp.zeros((1, LANES), jnp.float32)

    kf = len(RIGHT)

    def pad8(v):
        return jnp.concatenate([v, jnp.zeros((8 - rows, LANES), jnp.float32)], axis=0)

    def halo_in(l, carry):
        for side, names in enumerate((RIGHT, LEFT)):
            packed = pad8(xr[side, l])
            for k, i in enumerate(names):
                shift = (127 - k) if side == 0 else (LANES - k) % LANES
                post[i, l + 1, 0:rows, cols : cols + LANES] = pltpu.roll(packed, shift, 1)[0:rows]
        for side, names in enumerate((UP, DOWN)):
            row = 7 if side == 0 else rows
            for k, i in enumerate(names):
                post[i, l + 1, row : row + 1, 0:cols] = yr[side, l + k * layers + (1 if k else 0)]
        for n, (i, row, off) in enumerate(((7, 7, 0), (10, 7, 1), (8, rows, 0), (9, rows, 1))):
            post[i, l + 1, row : row + 1, cols : cols + LANES] = ds[n, l + off]
        return carry

    lax.fori_loop(0, layers, halo_in, 0)
    from_left = pltpu.roll(pad8(xr[0, 0]), 127 - kf, 1)
    from_right = pltpu.roll(pad8(xr[1, 0]), LANES - kf, 1)
    flags[0:rows, cols:] = jnp.where(lane < 64, from_right, from_left)[0:rows]
    flags[7:8, 0:cols] = yr[0, layers]
    flags[rows : rows + 1, 0:cols] = yr[1, layers]
    flags[7:8, cols:] = jnp.where(lane[:1] < 64, ds[1, 0], ds[0, layers])
    flags[rows : rows + 1, cols:] = jnp.where(lane[:1] < 64, ds[2, layers], ds[3, 0])

    wide = cols + LANES

    def shifted(v, cx, cy):
        if cy:
            v = pltpu.roll(v, 1 if cy > 0 else 7, 0)
        if cx:
            v = pltpu.roll(v, 1 if cx > 0 else wide - 1, 1)
        return v[0:rows, 0:cols]

    flag_all = flags[...]
    pulled_flag = {
        (cx, cy): shifted(flag_all, cx, cy) for cx in (-1, 0, 1) for cy in (-1, 0, 1)
        if cx == 0 or cy == 0 or True
    }
    me = own_flag > 0.5
    for cut in range(ngz - solid_ranks):
        vel[cut, 3 * thick] = own_flag

    def stream(l, cut, inner):
        out = []
        for i in range(19):
            cx, cy, cz = VEL19[i]
            span = wide if cx else cols
            src = shifted_span(post[i, l + 1 - cz, :, 0:span], cx, cy)
            flag = pulled_flag[cx, cy]
            if cz > 0:
                flag = jnp.where(l > 0, flag, 0.0)
            if cz < 0:
                flag = jnp.where(l < layers - 1, flag, 0.0)
            back = post[OPPOSITE[i], l + 1, 0:rows, 0:cols]
            got = jnp.where(flag > 0.5, src, back)
            out.append(jnp.where(me, got, pops[i, l]))
        for i in range(19):
            pops[i, l] = out[i]
        scale = own_flag / tree_sum(out)
        m = momentum(out)
        for k in range(3):
            vel[cut, k * thick + inner] = m[k] * scale

    def shifted_span(v, cx, cy):
        if cy:
            v = pltpu.roll(v, 1 if cy > 0 else 7, 0)
        if cx:
            v = pltpu.roll(v, 1 if cx > 0 else wide - 1, 1)
        return v[0:rows, 0:cols]

    vel_copies = []
    for cut in range(ngz - solid_ranks):
        def step(inner, carry, cut=cut):
            stream(cut * thick + inner, cut, inner)
            return carry

        lax.fori_loop(0, thick, step, 0)
        to = cut + solid_ranks
        copy = remote(
            vel.at[cut], vin.at[gz], vsend.at[cut], vrecv.at[gz], {"gx": gx, "gy": gy, "gz": to}
        )
        local = pltpu.make_async_copy(vel.at[cut], vin.at[gz], vloc)
        pl.when(gz != to)(copy.start)
        pl.when(gz == to)(local.start)
        vel_copies.append((copy, local, to))

    store_flow = pltpu.make_async_copy(
        pops, flow_hbm.at[:, pl.ds(BASE, layers)], out_sem.at[1]
    )
    store_flow.start()

    load_adj.wait()
    for copy, _, ok, dst in tcopies:
        pl.when(ok)(copy.wait_recv)

        @pl.when(jnp.logical_not(ok))
        def _():
            dst[...] = jnp.zeros(dst.shape, jnp.float32)

    tall = adj.shape[2]

    def pulled_at(t):
        v = [adj[0, t]]
        v.append(pltpu.roll(jnp.concatenate([adj[1, t], tx[0, t]], 1), wide - 1, 1)[:, 0:cols])
        v.append(pltpu.roll(jnp.concatenate([adj[2, t], tx[1, t]], 1), 1, 1)[:, 0:cols])
        v.append(pltpu.roll(jnp.concatenate([adj[3, t], ty[0, t]], 0), tall + 7, 0)[0:tall])
        v.append(pltpu.roll(jnp.concatenate([adj[4, t], ty[1, t]], 0), 1, 0)[0:tall])
        v.append(adj[5, t + 1] if t + 1 < thick else tz[0])
        v.append(adj[6, t - 1] if t > 0 else tz[1])
        return v

    def mean_of(v):
        return 0.25 * v[0] + 0.125 * tree_sum(v[1:])

    @pl.when(gz < solid_ranks)
    def _():
        @pl.when(gz == 0)
        def _():
            for other in range(1, ngz):
                remote(heat, hin.at[other], hsend, hrecv.at[other], peers[0]).wait_recv()
            hin[0] = heat[...]
        for t in range(thick):
            v = pulled_at(t)
            core = OMEGA_SOLID * mean_of(v)
            if t == 0:
                codes = jnp.concatenate([hin[g, 0] for g in range(ngz)], axis=0)
                hot = jnp.where(codes == 2.0, 1.0, 0.0)
                core = core + jnp.where(gz == 0, hot, 0.0)
            for j in range(7):
                prev[j, t] = (1.0 - OMEGA_SOLID) * v[j] + core

    @pl.when(gz >= solid_ranks)
    def _():
        for source in range(ngz):
            @pl.when(gz != source)
            def _():
                remote(vel.at[0], vin.at[source], vsend.at[0], vrecv.at[source], peers[0]).wait_recv()
        pltpu.make_async_copy(vel.at[0], vin.at[gz], vloc).wait()
        wet = jnp.concatenate([vin[g, 3 * thick] for g in range(ngz)], axis=0)
        omega = jnp.where(wet > 0.5, OMEGA_FLUID, OMEGA_SOLID)
        rest = 1.0 - omega
        for t in range(thick):
            v = pulled_at(t)
            u = [
                jnp.concatenate([vin[g, k * thick + t] for g in range(ngz)], axis=0)
                for k in range(3)
            ]
            carried = (
                u[0] * (v[1] - v[2]) + u[1] * (v[3] - v[4]) + u[2] * (v[5] - v[6])
            )
            core = omega * (mean_of(v) + 0.5 * carried)
            for j in range(7):
                prev[j, t] = rest * v[j] + core

    store_prev = pltpu.make_async_copy(prev, prev_hbm, out_sem.at[2])
    store_prev.start()

    for copy, ok, _ in flow_copies:
        pl.when(ok)(copy.wait_send)
    for copy, ok, _, _ in tcopies:
        pl.when(ok)(copy.wait_send)
    pl.when(gz > 0)(heat_send.wait_send)
    for copy, _, to in vel_copies:
        pl.when(gz != to)(copy.wait_send)
    keep_low.wait()
    store_flow.wait()
    store_prev.wait()


def per_device(sizes, populations, cell_type, adjoint):
    ngx, ngy, ngz = sizes
    depth, rows, cols = cell_type.shape
    layers = depth - BASE
    thick, tall = adjoint.shape[1:3]
    nsend = ngz - BASE // thick
    f32 = jnp.float32
    nrow = 5 * layers + 1
    vm = lambda *shape: pltpu.VMEM(shape, f32)
    dma = lambda *shape: pltpu.SemaphoreType.DMA(shape)
    return pl.pallas_call(
        functools.partial(kernel, (ngx, ngy, ngz, depth, rows, cols)),
        out_shape=(
            jax.ShapeDtypeStruct(populations.shape, f32),
            jax.ShapeDtypeStruct(adjoint.shape, f32),
        ),
        in_specs=[pl.BlockSpec(memory_space=pl.ANY)] * 3,
        out_specs=(pl.BlockSpec(memory_space=pl.ANY),) * 2,
        scratch_shapes=[
            vm(19, layers, rows, cols),
            pltpu.VMEM((2, rows, cols), jnp.int32),
            vm(*adjoint.shape),
            vm(19, layers + 2, 8, cols + LANES),
            vm(8, cols + LANES),
            vm(*adjoint.shape),
            vm(2, layers, rows, LANES),
            vm(2, layers, rows, LANES),
            vm(2, nrow, 1, cols),
            vm(2, nrow, 1, cols),
            vm(4, layers + 1, 1, LANES),
            vm(2, thick, tall, LANES),
            vm(2, thick, 8, cols),
            vm(2, tall, cols),
            vm(nsend, 3 * thick + 1, rows, cols),
            vm(ngz, 3 * thick + 1, rows, cols),
            vm(1, rows, cols),
            vm(ngz, 1, rows, cols),
            dma(4), dma(3), dma(8), dma(8), dma(6), dma(6),
            dma(nsend), dma(ngz), pltpu.SemaphoreType.DMA, dma(ngz), pltpu.SemaphoreType.DMA,
        ],
        compiler_params=pltpu.CompilerParams(
            collective_id=0, has_side_effects=True, vmem_limit_bytes=40 * 1024 * 1024
        ),
        name="flow_thermal",
    )(populations, cell_type, adjoint)


def solution(mesh):
    placed = (
        P(None, None, ("gy", "gz"), "gx"),
        P(None, ("gy", "gz"), "gx"),
        P(None, "gz", "gy", "gx"),
    )
    sizes = (mesh.shape["gx"], mesh.shape["gy"], mesh.shape["gz"])
    return jax.shard_map(
        functools.partial(per_device, sizes),
        mesh=mesh,
        in_specs=placed,
        out_specs=(P(None, None, ("gy", "gz"), "gx"), P(None, "gz", "gy", "gx")),
        check_vma=False,
    )
```

```python
import functools

import jax
import jax.numpy as jnp
from jax import lax
from jax.experimental import pallas as pl
from jax.experimental.pallas import tpu as pltpu
from jax.sharding import PartitionSpec as P

VEL19 = [
    (0, 0, 0), (1, 0, 0), (-1, 0, 0), (0, 1, 0), (0, -1, 0), (0, 0, 1), (0, 0, -1),
    (1, 1, 0), (-1, -1, 0), (1, -1, 0), (-1, 1, 0), (1, 0, 1), (-1, 0, -1), (1, 0, -1),
    (-1, 0, 1), (0, 1, 1), (0, -1, -1), (0, 1, -1), (0, -1, 1),
]
WEIGHT19 = [1.0 / 3.0] + [1.0 / 18.0] * 6 + [1.0 / 36.0] * 12
OPPOSITE = [0, 2, 1, 4, 3, 6, 5, 8, 7, 10, 9, 12, 11, 14, 13, 16, 15, 18, 17]
OMEGA_FLOW = 1.6
OMEGA_FLUID = 1.25
OMEGA_SOLID = 1.6
BASE = 8
LANES = 128
MESH = pl.DeviceIdType.MESH

RIGHT = [1, 7, 9, 11, 13]
LEFT = [2, 8, 10, 12, 14]
UP = [7, 10, 3, 15, 17]
DOWN = [8, 9, 4, 16, 18]


def tree_sum(terms):
    terms = list(terms)
    while len(terms) > 1:
        terms = [sum(terms[i : i + 2][1:], terms[i]) for i in range(0, len(terms), 2)]
    return terms[0]


def momentum(pops):
    out = []
    for k in range(3):
        plus = tree_sum([pops[i] for i in range(19) if VEL19[i][k] > 0])
        minus = tree_sum([pops[i] for i in range(19) if VEL19[i][k] < 0])
        out.append(plus - minus)
    return out


def kernel(
    sizes, pops_hbm, cell_hbm, adj_hbm, flow, vin, hin, tx, ty, tz,
    cells, post, flags, xs, xr, ys, yr, ds, vel, planes,
    in_sem, send_sem, recv_sem, tsend, trecv, vsend, vrecv, hsend, hrecv,
):
    ngx, ngy, ngz, depth, rows, cols = sizes
    layers = depth - BASE
    thick = depth // ngz
    solid_ranks = BASE // thick
    gx, gy, gz = lax.axis_index("gx"), lax.axis_index("gy"), lax.axis_index("gz")
    band = gy * ngz + gz
    nband = ngy * ngz

    def at(x, b):
        return {"gx": x, "gy": b // ngz, "gz": lax.rem(b, ngz)}

    has = {
        (1, 0): gx < ngx - 1, (-1, 0): gx > 0,
        (0, 1): band < nband - 1, (0, -1): band > 0,
    }
    for dx in (1, -1):
        for dy in (1, -1):
            has[dx, dy] = jnp.logical_and(has[dx, 0], has[0, dy])
    where_to = {key: at(gx + key[0], band + key[1]) for key in has}
    thermal_links = [
        (gx < ngx - 1, {"gx": gx + 1, "gy": gy, "gz": gz}),
        (gx > 0, {"gx": gx - 1, "gy": gy, "gz": gz}),
        (gy < ngy - 1, {"gx": gx, "gy": gy + 1, "gz": gz}),
        (gy > 0, {"gx": gx, "gy": gy - 1, "gz": gz}),
        (gz < ngz - 1, {"gx": gx, "gy": gy, "gz": gz + 1}),
        (gz > 0, {"gx": gx, "gy": gy, "gz": gz - 1}),
    ]
    peers = [{"gx": gx, "gy": gy, "gz": lax.rem(gz + k, ngz)} for k in range(1, ngz)]

    upper = pl.ds(BASE, layers)
    lower = pl.ds(0, BASE)
    load_pops = pltpu.make_async_copy(pops_hbm.at[:, upper], flow.at[:, upper], in_sem.at[0])
    load_top = pltpu.make_async_copy(cell_hbm.at[pl.ds(BASE, 1)], cells.at[pl.ds(0, 1)], in_sem.at[1])
    load_low = pltpu.make_async_copy(cell_hbm.at[pl.ds(0, 1)], cells.at[pl.ds(1, 1)], in_sem.at[2])
    load_rest = pltpu.make_async_copy(pops_hbm.at[:, lower], flow.at[:, lower], in_sem.at[3])
    load_top.start()
    load_low.start()
    load_pops.start()
    load_rest.start()

    barrier = pltpu.get_barrier_semaphore()
    total = jnp.int32(ngz - 1)
    for peer in peers:
        pl.semaphore_signal(barrier, inc=1, device_id=peer, device_id_type=MESH)
    links = [(has[key], where_to[key]) for key in has] + thermal_links[2:4]
    for ok, target in links:
        @pl.when(ok)
        def _():
            pl.semaphore_signal(barrier, inc=1, device_id=target, device_id_type=MESH)
        total = total + ok.astype(jnp.int32)

    load_top.wait()
    load_low.wait()
    load_pops.wait()
    own_flag = jnp.where(cells[0] == 0, 1.0, 0.0)
    flags[0:rows, 0:cols] = own_flag
    planes[0] = cells[1].astype(jnp.float32)
    planes[1] = cells[0].astype(jnp.float32)
    ys[0, layers] = own_flag[rows - 1 :]
    ys[1, layers] = own_flag[:1]
    lane = lax.broadcasted_iota(jnp.int32, (8, LANES), 1)

    def collide(l, carry):
        p = [flow[i, BASE + l] for i in range(19)]
        rho = tree_sum(p)
        m = momentum(p)
        inv = 1.0 / rho
        base = rho - 1.5 * (m[0] * m[0] + m[1] * m[1] + m[2] * m[2]) * inv
        inv45 = 4.5 * inv
        q = [None] * 19
        q[0] = (1.0 - OMEGA_FLOW) * p[0] + (OMEGA_FLOW * WEIGHT19[0]) * base
        for i in range(1, 19, 2):
            cm = tree_sum([m[k] if VEL19[i][k] > 0 else -m[k] for k in range(3) if VEL19[i][k]])
            even = base + inv45 * cm * cm
            odd = 3.0 * cm
            w = OMEGA_FLOW * WEIGHT19[i]
            q[i] = (1.0 - OMEGA_FLOW) * p[i] + w * (even + odd)
            q[i + 1] = (1.0 - OMEGA_FLOW) * p[i + 1] + w * (even - odd)
        for i in range(19):
            post[i, l + 1, 0:rows, 0:cols] = q[i]
        for side, (names, row) in enumerate(((UP, rows - 1), (DOWN, 0))):
            for k, i in enumerate(names):
                ys[side, l + k * layers + (1 if k else 0)] = q[i][row : row + 1]
        for side, names in enumerate((RIGHT, LEFT)):
            first = cols - LANES if side == 0 else 0
            edge = 1 if side == 0 else 0
            packed = jnp.zeros((8, LANES), jnp.float32)
            for k, i in enumerate(names):
                tile = post[i, l + 1, :, first : first + LANES]
                packed = jnp.where(lane == k, pltpu.roll(tile, (k + edge) % LANES, 1), packed)
            tile = flags[:, first : first + LANES]
            k = len(names)
            packed = jnp.where(lane == k, pltpu.roll(tile, (k + edge) % LANES, 1), packed)
            xs[side, l] = packed[0:rows]
        return carry

    lax.fori_loop(0, layers, collide, 0)

    pl.semaphore_wait(barrier, total)

    def remote(src, dst, ssem, rsem, target):
        return pltpu.make_async_remote_copy(
            src_ref=src, dst_ref=dst, send_sem=ssem, recv_sem=rsem,
            device_id=target, device_id_type=MESH,
        )

    last = pl.ds(cols - LANES, LANES)
    lead = pl.ds(0, LANES)
    jobs = [
        ((1, 0), xs.at[0], xr.at[0]),
        ((-1, 0), xs.at[1], xr.at[1]),
        ((0, 1), ys.at[0], yr.at[0]),
        ((0, -1), ys.at[1], yr.at[1]),
        ((1, 1), ys.at[0, pl.ds(0, layers + 1), :, last], ds.at[0]),
        ((-1, 1), ys.at[0, pl.ds(layers, layers + 1), :, lead], ds.at[1]),
        ((-1, -1), ys.at[1, pl.ds(0, layers + 1), :, lead], ds.at[2]),
        ((1, -1), ys.at[1, pl.ds(layers, layers + 1), :, last], ds.at[3]),
    ]
    flow_copies = []
    for n, (way, src, dst) in enumerate(jobs):
        copy = remote(src, dst, send_sem.at[n], recv_sem.at[n], where_to[way])
        flow_copies.append((copy, has[way], has[-way[0], -way[1]]))
    for copy, ok, _ in flow_copies:
        pl.when(ok)(copy.start)

    tcopies = []
    tjobs = [
        (1, adj_hbm.at[2, :, :, last], tx.at[1], 0),
        (0, adj_hbm.at[1, :, :, lead], tx.at[0], 1),
        (3, adj_hbm.at[4, :, pl.ds(adj_hbm.shape[2] - 8, 8), :], ty.at[1], 2),
        (2, adj_hbm.at[3, :, pl.ds(0, 8), :], ty.at[0], 3),
        (5, adj_hbm.at[6, thick - 1], tz.at[1], 4),
        (4, adj_hbm.at[5, 0], tz.at[0], 5),
    ]
    for sem, src, dst, link in tjobs:
        copy = remote(src, dst, tsend.at[sem], trecv.at[sem], thermal_links[link][1])
        tcopies.append((copy, thermal_links[link][0], thermal_links[link ^ 1][0], dst))
    for copy, ok, _, _ in tcopies:
        pl.when(ok)(copy.start)
    code_ranks = [0] + list(range(solid_ranks, ngz))
    code_copies = []
    for n, to in enumerate(code_ranks):
        copy = remote(
            planes.at[min(n, 1)], hin.at[gz], hsend.at[n], hrecv.at[gz],
            {"gx": gx, "gy": gy, "gz": to},
        )
        pl.when(gz != to)(copy.start)
        code_copies.append((copy, to))

        @pl.when(gz == to)
        def _():
            hin[gz] = planes[min(n, 1)]

    for n, (copy, _, ok) in enumerate(flow_copies):
        pl.when(ok)(copy.wait_recv)

        @pl.when(jnp.logical_not(ok))
        def _():
            if n < 2:
                xr[n, 0] = jnp.zeros((rows, LANES), jnp.float32)
            elif n < 4:
                yr[n - 2, layers] = jnp.zeros((1, cols), jnp.float32)
            else:
                ds[n - 4, layers if n % 2 == 0 else 0] = jnp.zeros((1, LANES), jnp.float32)

    kf = len(RIGHT)

    def pad8(v):
        return jnp.concatenate([v, jnp.zeros((8 - rows, LANES), jnp.float32)], axis=0)

    def halo_in(l, carry):
        for side, names in enumerate((RIGHT, LEFT)):
            packed = pad8(xr[side, l])
            for k, i in enumerate(names):
                shift = (127 - k) if side == 0 else (LANES - k) % LANES
                post[i, l + 1, 0:rows, cols : cols + LANES] = pltpu.roll(packed, shift, 1)[0:rows]
        for side, names in enumerate((UP, DOWN)):
            row = 7 if side == 0 else rows
            for k, i in enumerate(names):
                post[i, l + 1, row : row + 1, 0:cols] = yr[side, l + k * layers + (1 if k else 0)]
        for n, (i, row, off) in enumerate(((7, 7, 0), (10, 7, 1), (8, rows, 0), (9, rows, 1))):
            post[i, l + 1, row : row + 1, cols : cols + LANES] = ds[n, l + off]
        return carry

    lax.fori_loop(0, layers, halo_in, 0)
    from_left = pltpu.roll(pad8(xr[0, 0]), 127 - kf, 1)
    from_right = pltpu.roll(pad8(xr[1, 0]), LANES - kf, 1)
    flags[0:rows, cols:] = jnp.where(lane < 64, from_right, from_left)[0:rows]
    flags[7:8, 0:cols] = yr[0, layers]
    flags[rows : rows + 1, 0:cols] = yr[1, layers]
    flags[7:8, cols:] = jnp.where(lane[:1] < 64, ds[1, 0], ds[0, layers])
    flags[rows : rows + 1, cols:] = jnp.where(lane[:1] < 64, ds[2, layers], ds[3, 0])

    wide = cols + LANES

    def shifted(v, cx, cy):
        if cy:
            v = pltpu.roll(v, 1 if cy > 0 else 7, 0)
        if cx:
            v = pltpu.roll(v, 1 if cx > 0 else wide - 1, 1)
        return v[0:rows, 0:cols]

    flag_all = flags[...]
    pulled_flag = {
        (cx, cy): shifted(flag_all, cx, cy) for cx in (-1, 0, 1) for cy in (-1, 0, 1)
        if cx == 0 or cy == 0 or True
    }
    me = own_flag > 0.5
    def stream(l, slot, to):
        out = []
        for i in range(19):
            cx, cy, cz = VEL19[i]
            span = wide if cx else cols
            src = shifted_span(post[i, l + 1 - cz, :, 0:span], cx, cy)
            flag = pulled_flag[cx, cy]
            if cz > 0:
                flag = jnp.where(l > 0, flag, 0.0)
            if cz < 0:
                flag = jnp.where(l < layers - 1, flag, 0.0)
            back = post[OPPOSITE[i], l + 1, 0:rows, 0:cols]
            got = jnp.where(flag > 0.5, src, back)
            out.append(jnp.where(me, got, flow[i, BASE + l]))
        for i in range(19):
            flow[i, BASE + l] = out[i]
        scale = own_flag / tree_sum(out)
        m = momentum(out)
        for k in range(3):
            vel[l, k] = m[k] * scale
        copy = remote(
            vel.at[l], vin.at[gz, slot], vsend.at[to - solid_ranks], vrecv.at[gz],
            {"gx": gx, "gy": gy, "gz": to},
        )
        pl.when(gz != to)(copy.start)

        @pl.when(gz == to)
        def _():
            vin[gz, slot] = vel[l]

    def shifted_span(v, cx, cy):
        if cy:
            v = pltpu.roll(v, 1 if cy > 0 else 7, 0)
        if cx:
            v = pltpu.roll(v, 1 if cx > 0 else wide - 1, 1)
        return v[0:rows, 0:cols]

    for to in range(solid_ranks, ngz):
        def step(inner, carry, to=to):
            stream((to - solid_ranks) * thick + inner, inner, to)
            return carry

        lax.fori_loop(0, thick, step, 0)

    load_rest.wait()
    for copy, _, ok, dst in tcopies:
        pl.when(ok)(copy.wait_recv)

        @pl.when(jnp.logical_not(ok))
        def _():
            dst[...] = jnp.zeros(dst.shape, jnp.float32)

    for source in range(ngz):
        own = {"gx": gx, "gy": gy, "gz": lax.rem(gz + 1, ngz)}
        codes = remote(planes.at[0], hin.at[source], hsend.at[0], hrecv.at[source], own)
        moved = remote(
            vel.at[pl.ds(0, thick)], vin.at[source], vsend.at[0], vrecv.at[source], own
        )
        active = jnp.logical_and(gz >= solid_ranks, gz != source)
        pl.when(jnp.logical_or(active, jnp.logical_and(gz == 0, gz != source)))(codes.wait_recv)
        pl.when(active)(moved.wait_recv)

    for copy, ok, _ in flow_copies:
        pl.when(ok)(copy.wait_send)
    for copy, ok, _, _ in tcopies:
        pl.when(ok)(copy.wait_send)
    for copy, to in code_copies:
        pl.when(gz != to)(copy.wait_send)
    for to in range(solid_ranks, ngz):
        first = (to - solid_ranks) * thick
        sent = remote(
            vel.at[pl.ds(first, thick)], vin.at[0], vsend.at[to - solid_ranks], vrecv.at[0],
            {"gx": gx, "gy": gy, "gz": to},
        )
        pl.when(gz != to)(sent.wait_send)


def thermal_kernel(
    sizes, flow, adj, vin, hin, tx, ty, tz, flow_hbm, prev_hbm, prev, out_sem,
):
    ngz, solid_ranks = sizes
    gz = lax.axis_index("gz")
    thick, tall, cols = adj.shape[1:]
    wide = cols + LANES
    store_flow = pltpu.make_async_copy(flow, flow_hbm, out_sem.at[0])
    store_flow.start()

    def pulled_at(t):
        v = [adj[0, t]]
        v.append(pltpu.roll(jnp.concatenate([adj[1, t], tx[0, t]], 1), wide - 1, 1)[:, 0:cols])
        v.append(pltpu.roll(jnp.concatenate([adj[2, t], tx[1, t]], 1), 1, 1)[:, 0:cols])
        v.append(pltpu.roll(jnp.concatenate([adj[3, t], ty[0, t]], 0), tall + 7, 0)[0:tall])
        v.append(pltpu.roll(jnp.concatenate([adj[4, t], ty[1, t]], 0), 1, 0)[0:tall])
        v.append(adj[5, t + 1] if t + 1 < thick else tz[0])
        v.append(adj[6, t - 1] if t > 0 else tz[1])
        return v

    def mean_of(v):
        return 0.25 * v[0] + 0.125 * tree_sum(v[1:])

    def gathered(pick):
        return jnp.concatenate([pick(g) for g in range(ngz)], axis=0)

    @pl.when(gz < solid_ranks)
    def _():
        for t in range(thick):
            v = pulled_at(t)
            core = OMEGA_SOLID * mean_of(v)
            if t == 0:
                hot = jnp.where(gathered(lambda g: hin[g]) == 2.0, 1.0, 0.0)
                core = core + jnp.where(gz == 0, hot, 0.0)
            for j in range(7):
                prev[j, t] = (1.0 - OMEGA_SOLID) * v[j] + core

    @pl.when(gz >= solid_ranks)
    def _():
        omega = jnp.where(gathered(lambda g: hin[g]) == 0.0, OMEGA_FLUID, OMEGA_SOLID)
        rest = 1.0 - omega
        for t in range(thick):
            v = pulled_at(t)
            u = [gathered(lambda g: vin[g, t, k]) for k in range(3)]
            carried = u[0] * (v[1] - v[2]) + u[1] * (v[3] - v[4]) + u[2] * (v[5] - v[6])
            core = omega * (mean_of(v) + 0.5 * carried)
            for j in range(7):
                prev[j, t] = rest * v[j] + core

    store_prev = pltpu.make_async_copy(prev, prev_hbm, out_sem.at[1])
    store_prev.start()
    store_flow.wait()
    store_prev.wait()


def per_device(sizes, populations, cell_type, adjoint):
    ngx, ngy, ngz = sizes
    depth, rows, cols = cell_type.shape
    layers = depth - BASE
    thick, tall = adjoint.shape[1:3]
    nsend = ngz - BASE // thick
    f32 = jnp.float32
    nrow = 5 * layers + 1
    vm = lambda *shape: pltpu.VMEM(shape, f32)
    dma = lambda *shape: pltpu.SemaphoreType.DMA(shape)
    held = lambda *shape: jax.ShapeDtypeStruct(shape, f32)
    hbm = pl.BlockSpec(memory_space=pltpu.HBM)
    vmem = pl.BlockSpec(memory_space=pltpu.VMEM)
    parts = pl.pallas_call(
        functools.partial(kernel, (ngx, ngy, ngz, depth, rows, cols)),
        out_shape=(
            held(*populations.shape),
            held(ngz, thick, 3, rows, cols),
            held(ngz, rows, cols),
            held(2, thick, tall, LANES),
            held(2, thick, 8, cols),
            held(2, tall, cols),
        ),
        in_specs=[hbm] * 3,
        out_specs=(vmem,) * 6,
        scratch_shapes=[
            pltpu.VMEM((2, rows, cols), jnp.int32),
            vm(19, layers + 2, 8, cols + LANES),
            vm(8, cols + LANES),
            vm(2, layers, rows, LANES),
            vm(2, layers, rows, LANES),
            vm(2, nrow, 1, cols),
            vm(2, nrow, 1, cols),
            vm(4, layers + 1, 1, LANES),
            vm(layers, 3, rows, cols),
            vm(2, rows, cols),
            dma(4), dma(8), dma(8), dma(6), dma(6),
            dma(nsend), dma(ngz), dma(nsend + 1), dma(ngz),
        ],
        compiler_params=pltpu.CompilerParams(
            collective_id=0, has_side_effects=True, vmem_limit_bytes=24 * 1024 * 1024
        ),
        name="flow_step",
    )(*[pltpu.with_memory_space_constraint(x, pltpu.HBM) for x in (populations, cell_type, adjoint)])
    flow, vin, hin, tx, ty, tz = parts
    return pl.pallas_call(
        functools.partial(thermal_kernel, (ngz, BASE // thick)),
        out_shape=(held(*populations.shape), held(*adjoint.shape)),
        in_specs=[vmem] * 7,
        out_specs=(hbm, hbm),
        scratch_shapes=[vm(*adjoint.shape), dma(2)],
        compiler_params=pltpu.CompilerParams(vmem_limit_bytes=16 * 1024 * 1024),
        name="thermal_step",
    )(flow, adjoint, vin, hin, tx, ty, tz)


def solution(mesh):
    placed = (
        P(None, None, ("gy", "gz"), "gx"),
        P(None, ("gy", "gz"), "gx"),
        P(None, "gz", "gy", "gx"),
    )
    sizes = (mesh.shape["gx"], mesh.shape["gy"], mesh.shape["gz"])
    return jax.shard_map(
        functools.partial(per_device, sizes),
        mesh=mesh,
        in_specs=placed,
        out_specs=(P(None, None, ("gy", "gz"), "gx"), P(None, "gz", "gy", "gx")),
        check_vma=False,
    )
```

```python
import functools

import jax
import jax.numpy as jnp
from jax import lax
from jax.experimental import pallas as pl
from jax.experimental.pallas import tpu as pltpu
from jax.sharding import PartitionSpec as P

VEL19 = [
    (0, 0, 0), (1, 0, 0), (-1, 0, 0), (0, 1, 0), (0, -1, 0), (0, 0, 1), (0, 0, -1),
    (1, 1, 0), (-1, -1, 0), (1, -1, 0), (-1, 1, 0), (1, 0, 1), (-1, 0, -1), (1, 0, -1),
    (-1, 0, 1), (0, 1, 1), (0, -1, -1), (0, 1, -1), (0, -1, 1),
]
WEIGHT19 = [1.0 / 3.0] + [1.0 / 18.0] * 6 + [1.0 / 36.0] * 12
OPPOSITE = [0, 2, 1, 4, 3, 6, 5, 8, 7, 10, 9, 12, 11, 14, 13, 16, 15, 18, 17]
OMEGA_FLOW = 1.6
OMEGA_FLUID = 1.25
OMEGA_SOLID = 1.6
BASE = 8
LANES = 128
MESH = pl.DeviceIdType.MESH

RIGHT = [1, 7, 9, 11, 13]
LEFT = [2, 8, 10, 12, 14]
UP = [7, 10, 3, 15, 17]
DOWN = [8, 9, 4, 16, 18]


def tree_sum(terms):
    terms = list(terms)
    while len(terms) > 1:
        terms = [sum(terms[i : i + 2][1:], terms[i]) for i in range(0, len(terms), 2)]
    return terms[0]


def momentum(pops):
    out = []
    for k in range(3):
        plus = tree_sum([pops[i] for i in range(19) if VEL19[i][k] > 0])
        minus = tree_sum([pops[i] for i in range(19) if VEL19[i][k] < 0])
        out.append(plus - minus)
    return out


def kernel(
    sizes, pops_hbm, cell_hbm, adj_hbm, flow, vin, hin, tx, ty, tz,
    cells, post, flags, xs, xr, ys, yr, ds, vel, planes,
    in_sem, send_sem, recv_sem, tsend, trecv, vsend, vrecv, hsend, hrecv,
):
    ngx, ngy, ngz, depth, rows, cols = sizes
    layers = depth - BASE
    thick = depth // ngz
    solid_ranks = BASE // thick
    gx, gy, gz = lax.axis_index("gx"), lax.axis_index("gy"), lax.axis_index("gz")
    band = gy * ngz + gz
    nband = ngy * ngz

    def at(x, b):
        return {"gx": x, "gy": b // ngz, "gz": lax.rem(b, ngz)}

    has = {
        (1, 0): gx < ngx - 1, (-1, 0): gx > 0,
        (0, 1): band < nband - 1, (0, -1): band > 0,
    }
    for dx in (1, -1):
        for dy in (1, -1):
            has[dx, dy] = jnp.logical_and(has[dx, 0], has[0, dy])
    where_to = {key: at(gx + key[0], band + key[1]) for key in has}
    thermal_links = [
        (gx < ngx - 1, {"gx": gx + 1, "gy": gy, "gz": gz}),
        (gx > 0, {"gx": gx - 1, "gy": gy, "gz": gz}),
        (gy < ngy - 1, {"gx": gx, "gy": gy + 1, "gz": gz}),
        (gy > 0, {"gx": gx, "gy": gy - 1, "gz": gz}),
        (gz < ngz - 1, {"gx": gx, "gy": gy, "gz": gz + 1}),
        (gz > 0, {"gx": gx, "gy": gy, "gz": gz - 1}),
    ]
    peers = [{"gx": gx, "gy": gy, "gz": lax.rem(gz + k, ngz)} for k in range(1, ngz)]

    upper = pl.ds(BASE, layers)
    lower = pl.ds(0, BASE)
    load_pops = pltpu.make_async_copy(pops_hbm.at[:, upper], flow.at[:, upper], in_sem.at[0])
    load_top = pltpu.make_async_copy(cell_hbm.at[pl.ds(BASE, 1)], cells.at[pl.ds(0, 1)], in_sem.at[1])
    load_low = pltpu.make_async_copy(cell_hbm.at[pl.ds(0, 1)], cells.at[pl.ds(1, 1)], in_sem.at[2])
    load_rest = pltpu.make_async_copy(pops_hbm.at[:, lower], flow.at[:, lower], in_sem.at[3])
    barrier = pltpu.get_barrier_semaphore()
    total = jnp.int32(ngz - 1)
    links = [(has[key], where_to[key]) for key in reversed(list(has))] + thermal_links[2:4]
    for ok, target in links:
        @pl.when(ok)
        def _():
            pl.semaphore_signal(barrier, inc=1, device_id=target, device_id_type=MESH)
        total = total + ok.astype(jnp.int32)
    for peer in peers:
        pl.semaphore_signal(barrier, inc=1, device_id=peer, device_id_type=MESH)

    load_top.start()
    load_low.start()
    load_pops.start()
    load_rest.start()

    load_top.wait()
    load_low.wait()
    load_pops.wait()
    own_flag = jnp.where(cells[0] == 0, 1.0, 0.0)
    flags[0:rows, 0:cols] = own_flag
    planes[0] = cells[1].astype(jnp.float32)
    planes[1] = cells[0].astype(jnp.float32)
    ys[0, layers] = own_flag[rows - 1 :]
    ys[1, layers] = own_flag[:1]
    lane = lax.broadcasted_iota(jnp.int32, (8, LANES), 1)

    def collide(l, carry):
        p = [flow[i, BASE + l] for i in range(19)]
        rho = tree_sum(p)
        m = momentum(p)
        inv = 1.0 / rho
        base = rho - 1.5 * (m[0] * m[0] + m[1] * m[1] + m[2] * m[2]) * inv
        inv45 = 4.5 * inv
        q = [None] * 19
        q[0] = (1.0 - OMEGA_FLOW) * p[0] + (OMEGA_FLOW * WEIGHT19[0]) * base
        for i in range(1, 19, 2):
            cm = tree_sum([m[k] if VEL19[i][k] > 0 else -m[k] for k in range(3) if VEL19[i][k]])
            even = base + inv45 * cm * cm
            odd = 3.0 * cm
            w = OMEGA_FLOW * WEIGHT19[i]
            q[i] = (1.0 - OMEGA_FLOW) * p[i] + w * (even + odd)
            q[i + 1] = (1.0 - OMEGA_FLOW) * p[i + 1] + w * (even - odd)
        for i in range(19):
            post[i, l + 1, 0:rows, 0:cols] = q[i]
        for side, (names, row) in enumerate(((UP, rows - 1), (DOWN, 0))):
            for k, i in enumerate(names):
                ys[side, l + k * layers + (1 if k else 0)] = q[i][row : row + 1]
        for side, names in enumerate((RIGHT, LEFT)):
            first = cols - LANES if side == 0 else 0
            edge = 1 if side == 0 else 0
            packed = jnp.zeros((8, LANES), jnp.float32)
            for k, i in enumerate(names):
                tile = post[i, l + 1, :, first : first + LANES]
                packed = jnp.where(lane == k, pltpu.roll(tile, (k + edge) % LANES, 1), packed)
            tile = flags[:, first : first + LANES]
            k = len(names)
            packed = jnp.where(lane == k, pltpu.roll(tile, (k + edge) % LANES, 1), packed)
            xs[side, l] = packed[0:rows]
        return carry

    lax.fori_loop(0, layers, collide, 0, unroll=2)

    pl.semaphore_wait(barrier, total)

    def remote(src, dst, ssem, rsem, target):
        return pltpu.make_async_remote_copy(
            src_ref=src, dst_ref=dst, send_sem=ssem, recv_sem=rsem,
            device_id=target, device_id_type=MESH,
        )

    last = pl.ds(cols - LANES, LANES)
    lead = pl.ds(0, LANES)
    jobs = [
        ((1, 0), xs.at[0], xr.at[0]),
        ((-1, 0), xs.at[1], xr.at[1]),
        ((0, 1), ys.at[0], yr.at[0]),
        ((0, -1), ys.at[1], yr.at[1]),
        ((1, 1), ys.at[0, pl.ds(0, layers + 1), :, last], ds.at[0]),
        ((-1, 1), ys.at[0, pl.ds(layers, layers + 1), :, lead], ds.at[1]),
        ((-1, -1), ys.at[1, pl.ds(0, layers + 1), :, lead], ds.at[2]),
        ((1, -1), ys.at[1, pl.ds(layers, layers + 1), :, last], ds.at[3]),
    ]
    flow_copies = []
    for n, (way, src, dst) in enumerate(jobs):
        copy = remote(src, dst, send_sem.at[n], recv_sem.at[n], where_to[way])
        flow_copies.append((copy, has[way], has[-way[0], -way[1]]))
    for n in (4, 5, 6, 7, 2, 3, 0, 1):
        copy, ok, _ = flow_copies[n]
        pl.when(ok)(copy.start)

    tcopies = []
    tjobs = [
        (1, adj_hbm.at[2, :, :, last], tx.at[1], 0),
        (0, adj_hbm.at[1, :, :, lead], tx.at[0], 1),
        (3, adj_hbm.at[4, :, pl.ds(adj_hbm.shape[2] - 8, 8), :], ty.at[1], 2),
        (2, adj_hbm.at[3, :, pl.ds(0, 8), :], ty.at[0], 3),
        (5, adj_hbm.at[6, thick - 1], tz.at[1], 4),
        (4, adj_hbm.at[5, 0], tz.at[0], 5),
    ]
    for sem, src, dst, link in tjobs:
        copy = remote(src, dst, tsend.at[sem], trecv.at[sem], thermal_links[link][1])
        tcopies.append((copy, thermal_links[link][0], thermal_links[link ^ 1][0], dst))
    for copy, ok, _, _ in tcopies:
        pl.when(ok)(copy.start)
    code_ranks = [0] + list(range(solid_ranks, ngz))
    code_copies = []
    for n, to in enumerate(code_ranks):
        copy = remote(
            planes.at[min(n, 1)], hin.at[gz], hsend.at[n], hrecv.at[gz],
            {"gx": gx, "gy": gy, "gz": to},
        )
        pl.when(gz != to)(copy.start)
        code_copies.append((copy, to))

        @pl.when(gz == to)
        def _():
            hin[gz] = planes[min(n, 1)]

    kf = len(RIGHT)

    def pad8(v):
        return jnp.concatenate([v, jnp.zeros((8 - rows, LANES), jnp.float32)], axis=0)

    def arrive(n):
        copy, _, ok = flow_copies[n]
        pl.when(ok)(copy.wait_recv)

        @pl.when(jnp.logical_not(ok))
        def _():
            if n < 2:
                xr[n, 0] = jnp.zeros((rows, LANES), jnp.float32)
            elif n < 4:
                yr[n - 2, layers] = jnp.zeros((1, cols), jnp.float32)
            else:
                ds[n - 4, layers if n % 2 == 0 else 0] = jnp.zeros((1, LANES), jnp.float32)

    for side, names in enumerate((RIGHT, LEFT)):
        arrive(side)
        def columns(l, carry, side=side, names=names):
            packed = pad8(xr[side, l])
            for k, i in enumerate(names):
                shift = (127 - k) if side == 0 else (LANES - k) % LANES
                post[i, l + 1, 0:rows, cols : cols + LANES] = pltpu.roll(packed, shift, 1)[0:rows]
            return carry

        lax.fori_loop(0, layers, columns, 0, unroll=2)
    for side, names in enumerate((UP, DOWN)):
        arrive(2 + side)
        row = 7 if side == 0 else rows
        def edge_rows(l, carry, side=side, names=names, row=row):
            for k, i in enumerate(names):
                post[i, l + 1, row : row + 1, 0:cols] = yr[side, l + k * layers + (1 if k else 0)]
            return carry

        lax.fori_loop(0, layers, edge_rows, 0, unroll=2)
    for n, (i, row, off) in enumerate(((7, 7, 0), (10, 7, 1), (8, rows, 0), (9, rows, 1))):
        arrive(4 + n)
        for l in range(layers):
            post[i, l + 1, row : row + 1, cols : cols + LANES] = ds[n, l + off]
    from_left = pltpu.roll(pad8(xr[0, 0]), 127 - kf, 1)
    from_right = pltpu.roll(pad8(xr[1, 0]), LANES - kf, 1)
    flags[0:rows, cols:] = jnp.where(lane < 64, from_right, from_left)[0:rows]
    flags[7:8, 0:cols] = yr[0, layers]
    flags[rows : rows + 1, 0:cols] = yr[1, layers]
    flags[7:8, cols:] = jnp.where(lane[:1] < 64, ds[1, 0], ds[0, layers])
    flags[rows : rows + 1, cols:] = jnp.where(lane[:1] < 64, ds[2, layers], ds[3, 0])

    wide = cols + LANES

    def shifted(v, cx, cy):
        if cy:
            v = pltpu.roll(v, 1 if cy > 0 else 7, 0)
        if cx:
            v = pltpu.roll(v, 1 if cx > 0 else wide - 1, 1)
        return v[0:rows, 0:cols]

    flag_all = flags[...]
    pulled_flag = {
        (cx, cy): shifted(flag_all, cx, cy) for cx in (-1, 0, 1) for cy in (-1, 0, 1)
        if cx == 0 or cy == 0 or True
    }
    me = own_flag > 0.5
    def stream(l, slot, to):
        out = []
        for i in range(19):
            cx, cy, cz = VEL19[i]
            span = wide if cx else cols
            src = shifted_span(post[i, l + 1 - cz, :, 0:span], cx, cy)
            flag = pulled_flag[cx, cy]
            if cz > 0:
                flag = jnp.where(l > 0, flag, 0.0)
            if cz < 0:
                flag = jnp.where(l < layers - 1, flag, 0.0)
            back = post[OPPOSITE[i], l + 1, 0:rows, 0:cols]
            got = jnp.where(flag > 0.5, src, back)
            out.append(jnp.where(me, got, flow[i, BASE + l]))
        for i in range(19):
            flow[i, BASE + l] = out[i]
        scale = own_flag / tree_sum(out)
        m = momentum(out)
        for k in range(3):
            vel[l, k] = m[k] * scale
        copy = remote(
            vel.at[l], vin.at[gz, slot], vsend.at[to - solid_ranks], vrecv.at[gz],
            {"gx": gx, "gy": gy, "gz": to},
        )
        pl.when(gz != to)(copy.start)

        @pl.when(gz == to)
        def _():
            vin[gz, slot] = vel[l]

    def shifted_span(v, cx, cy):
        if cy:
            v = pltpu.roll(v, 1 if cy > 0 else 7, 0)
        if cx:
            v = pltpu.roll(v, 1 if cx > 0 else wide - 1, 1)
        return v[0:rows, 0:cols]

    for to in range(solid_ranks, ngz):
        def step(inner, carry, to=to):
            stream((to - solid_ranks) * thick + inner, inner, to)
            return carry

        lax.fori_loop(0, thick, step, 0)

    load_rest.wait()
    for copy, _, ok, dst in tcopies:
        pl.when(ok)(copy.wait_recv)

        @pl.when(jnp.logical_not(ok))
        def _():
            dst[...] = jnp.zeros(dst.shape, jnp.float32)

    for source in range(ngz):
        own = {"gx": gx, "gy": gy, "gz": lax.rem(gz + 1, ngz)}
        codes = remote(planes.at[0], hin.at[source], hsend.at[0], hrecv.at[source], own)
        moved = remote(
            vel.at[pl.ds(0, thick)], vin.at[source], vsend.at[0], vrecv.at[source], own
        )
        active = jnp.logical_and(gz >= solid_ranks, gz != source)
        pl.when(jnp.logical_or(active, jnp.logical_and(gz == 0, gz != source)))(codes.wait_recv)
        pl.when(active)(moved.wait_recv)

    for copy, ok, _ in flow_copies:
        pl.when(ok)(copy.wait_send)
    for copy, ok, _, _ in tcopies:
        pl.when(ok)(copy.wait_send)
    for copy, to in code_copies:
        pl.when(gz != to)(copy.wait_send)
    for to in range(solid_ranks, ngz):
        first = (to - solid_ranks) * thick
        sent = remote(
            vel.at[pl.ds(first, thick)], vin.at[0], vsend.at[to - solid_ranks], vrecv.at[0],
            {"gx": gx, "gy": gy, "gz": to},
        )
        pl.when(gz != to)(sent.wait_send)


def thermal_kernel(
    sizes, flow, adj, vin, hin, tx, ty, tz, flow_hbm, prev_hbm, prev, flow_sem, prev_sem,
):
    ngz, solid_ranks = sizes
    gz = lax.axis_index("gz")
    thick, tall, cols = adj.shape[1:]
    wide = cols + LANES
    store_flow = pltpu.make_async_copy(flow, flow_hbm, flow_sem)
    store_flow.start()
    stores = [
        pltpu.make_async_copy(prev.at[:, t], prev_hbm.at[:, t], prev_sem.at[t])
        for t in range(thick)
    ]

    def pulled_at(t):
        v = [adj[0, t]]
        v.append(pltpu.roll(jnp.concatenate([adj[1, t], tx[0, t]], 1), wide - 1, 1)[:, 0:cols])
        v.append(pltpu.roll(jnp.concatenate([adj[2, t], tx[1, t]], 1), 1, 1)[:, 0:cols])
        v.append(pltpu.roll(jnp.concatenate([adj[3, t], ty[0, t]], 0), tall + 7, 0)[0:tall])
        v.append(pltpu.roll(jnp.concatenate([adj[4, t], ty[1, t]], 0), 1, 0)[0:tall])
        v.append(adj[5, t + 1] if t + 1 < thick else tz[0])
        v.append(adj[6, t - 1] if t > 0 else tz[1])
        return v

    def mean_of(v):
        return 0.25 * v[0] + 0.125 * tree_sum(v[1:])

    def gathered(pick):
        return jnp.concatenate([pick(g) for g in range(ngz)], axis=0)

    @pl.when(gz < solid_ranks)
    def _():
        for t in range(thick):
            v = pulled_at(t)
            core = OMEGA_SOLID * mean_of(v)
            if t == 0:
                hot = jnp.where(gathered(lambda g: hin[g]) == 2.0, 1.0, 0.0)
                core = core + jnp.where(gz == 0, hot, 0.0)
            for j in range(7):
                prev[j, t] = (1.0 - OMEGA_SOLID) * v[j] + core
            stores[t].start()

    @pl.when(gz >= solid_ranks)
    def _():
        omega = jnp.where(gathered(lambda g: hin[g]) == 0.0, OMEGA_FLUID, OMEGA_SOLID)
        rest = 1.0 - omega
        for t in range(thick):
            v = pulled_at(t)
            u = [gathered(lambda g: vin[g, t, k]) for k in range(3)]
            carried = u[0] * (v[1] - v[2]) + u[1] * (v[3] - v[4]) + u[2] * (v[5] - v[6])
            core = omega * (mean_of(v) + 0.5 * carried)
            for j in range(7):
                prev[j, t] = rest * v[j] + core
            stores[t].start()

    for store in stores:
        store.wait()
    store_flow.wait()


def per_device(sizes, populations, cell_type, adjoint):
    ngx, ngy, ngz = sizes
    depth, rows, cols = cell_type.shape
    layers = depth - BASE
    thick, tall = adjoint.shape[1:3]
    nsend = ngz - BASE // thick
    f32 = jnp.float32
    nrow = 5 * layers + 1
    vm = lambda *shape: pltpu.VMEM(shape, f32)
    dma = lambda *shape: pltpu.SemaphoreType.DMA(shape)
    held = lambda *shape: jax.ShapeDtypeStruct(shape, f32)
    hbm = pl.BlockSpec(memory_space=pltpu.HBM)
    vmem = pl.BlockSpec(memory_space=pltpu.VMEM)
    parts = pl.pallas_call(
        functools.partial(kernel, (ngx, ngy, ngz, depth, rows, cols)),
        out_shape=(
            held(*populations.shape),
            held(ngz, thick, 3, rows, cols),
            held(ngz, rows, cols),
            held(2, thick, tall, LANES),
            held(2, thick, 8, cols),
            held(2, tall, cols),
        ),
        in_specs=[hbm] * 3,
        out_specs=(vmem,) * 6,
        scratch_shapes=[
            pltpu.VMEM((2, rows, cols), jnp.int32),
            vm(19, layers + 2, 8, cols + LANES),
            vm(8, cols + LANES),
            vm(2, layers, rows, LANES),
            vm(2, layers, rows, LANES),
            vm(2, nrow, 1, cols),
            vm(2, nrow, 1, cols),
            vm(4, layers + 1, 1, LANES),
            vm(layers, 3, rows, cols),
            vm(2, rows, cols),
            dma(4), dma(8), dma(8), dma(6), dma(6),
            dma(nsend), dma(ngz), dma(nsend + 1), dma(ngz),
        ],
        compiler_params=pltpu.CompilerParams(
            collective_id=0, has_side_effects=True, vmem_limit_bytes=24 * 1024 * 1024
        ),
        name="flow_step",
    )(*[pltpu.with_memory_space_constraint(x, pltpu.HBM) for x in (populations, cell_type, adjoint)])
    flow, vin, hin, tx, ty, tz = parts
    return pl.pallas_call(
        functools.partial(thermal_kernel, (ngz, BASE // thick)),
        out_shape=(held(*populations.shape), held(*adjoint.shape)),
        in_specs=[vmem] * 7,
        out_specs=(hbm, hbm),
        scratch_shapes=[vm(*adjoint.shape), pltpu.SemaphoreType.DMA, dma(thick)],
        compiler_params=pltpu.CompilerParams(vmem_limit_bytes=16 * 1024 * 1024),
        name="thermal_step",
    )(flow, adjoint, vin, hin, tx, ty, tz)


def solution(mesh):
    placed = (
        P(None, None, ("gy", "gz"), "gx"),
        P(None, ("gy", "gz"), "gx"),
        P(None, "gz", "gy", "gx"),
    )
    sizes = (mesh.shape["gx"], mesh.shape["gy"], mesh.shape["gz"])
    return jax.shard_map(
        functools.partial(per_device, sizes),
        mesh=mesh,
        in_specs=placed,
        out_specs=(P(None, None, ("gy", "gz"), "gx"), P(None, "gz", "gy", "gx")),
        check_vma=False,
    )
```
